32 devices in a mesh: lat: 8 (over z, y), lon: 4 (over x, core).
Axes of the slice: x: 2, y: 2, z: 4, core: 2. Of those that a mesh axis runs over, the one named last changes fastest.
Arguments:
- state: bfloat16 [48, 1440, 512], P('lat', 'lon'), may hold values from -6 to 6
- filter_values: float32 [3, 48, 3, 8], replicated, may hold values from -2 to 2
- offsets: int32 [48, 3, 8], replicated, may hold values from -720 to 719, as said below
- mixing: bfloat16 [3, 512, 512], replicated, may hold values from -0.15625 to 0.15625
- cotangent: bfloat16 [48, 1440, 512], P('lat', 'lon'), may hold values from -6 to 6
Outputs:
- output: bfloat16 [48, 1440, 512], P('lat', 'lon')
- mixing_grad: float32 [3, 512, 512], P(None, 'lat', 'lon')
- state_grad: bfloat16 [48, 1440, 512], P('lat', 'lon')
The draws below stay inside these ranges and needn't reach their ends.
Inputs may be any that keep to these rules, and one draw needn't show every extreme that they name: On cycles i with i < 1 or i >= 47 an offset may reach half the cycle; on all other cycles -16 <= offsets[i, d, s] <= 16, and both 16 and -16 occur there.
All inputs are finite; a program needn't handle non-finite values.
Results may differ from the reference program's by a relative error of at most 0.0055.
Values may be sent and summed in bfloat16 or wider, within the bound.
A program may use at most 192 MiB of HBM per device.

```python
import jax
import jax.numpy as jnp
from jax import lax

C = 512
K = 3
NLON = 1440
NTAP = 8
HALO = 16
POLAR = 1
NLAT = 48


def draw_offsets(key, part):
    key = jax.random.fold_in(key, 7)
    near_key, far_key = jax.random.split(key)
    cycle_ids = jnp.arange(NLAT, dtype=jnp.int32)[:, None, None]
    polar = (cycle_ids < POLAR) | (cycle_ids >= NLAT - POLAR)
    near = jax.random.randint(near_key, (NLAT, 3, NTAP), -HALO, HALO + 1, dtype=jnp.int32)
    far = jax.random.randint(far_key, (NLAT, 3, NTAP), -(NLON // 2), NLON // 2, dtype=jnp.int32)
    values = jnp.where(polar, far, near)
    values = values.at[0, 1, 0].set(-(NLON // 2))
    values = values.at[0, 1, 1].set(NLON // 2 - 1)
    values = values.at[POLAR, 1, 0].set(HALO)
    values = values.at[POLAR, 1, 1].set(-HALO)
    return values


def block_scale(stream_key, extent, pieces, low, top_value):
    level = 1.0
    for axis_at, parts in pieces:
        draws = jax.random.uniform(jax.random.fold_in(jax.random.fold_in(stream_key, 6), axis_at), (parts,), jnp.float32, low / len(pieces), top_value / len(pieces))
        level = level * jnp.repeat(jnp.exp(draws), extent[axis_at] // parts).reshape((-1,) + (1,) * (len(extent) - 1 - axis_at))
    return level


def centred(rng, dims, scale, reach, pieces=(), kind=jnp.bfloat16):
    factor_of = block_scale(rng, dims, pieces, -0.22, 0.18) if pieces else 1.0
    result = jax.random.normal(rng, dims, jnp.float32) * scale * factor_of
    return jnp.minimum(jnp.maximum(result, -reach), reach).astype(kind)


def setup_inputs(seed: int = 0) -> dict:
    key_list = jax.random.split(jax.random.key(seed), 6)
    return {
        "state": centred(key_list[0], (NLAT, NLON, C), 1.0, 6.0, ((0, 8), (1, 4))),
        "filter_values": centred(key_list[1], (K, NLAT, 3, NTAP), ((3 * NTAP) ** -0.5), 2.0, (), jnp.float32),
        "offsets": draw_offsets(jax.random.fold_in(key_list[5], 71), 0),
        "mixing": centred(key_list[3], (K, C, C), (K * C) ** -0.5, 0.15625),
        "cotangent": centred(key_list[4], (NLAT, NLON, C), 1.0, 6.0, ((0, 8), (1, 4))),
    }


def gelu_value(value):
    return 0.5 * value * (1.0 + jax.scipy.special.erf(value * 0.7071067811865476))

def gelu_slope(value):
    rising = 0.5 * (1.0 + jax.scipy.special.erf(value * 0.7071067811865476))
    return rising + value * jnp.exp(-0.5 * value * value) * 0.3989422804014327

def reference(state, filter_values, offsets, mixing, cotangent):
    padded = jnp.pad(state, ((1, 1), (0, 0), (0, 0)))
    psi_pad = jnp.pad(filter_values, ((0, 0), (1, 1), (0, 0), (0, 0)))
    off_pad = jnp.pad(offsets, ((1, 1), (0, 0), (0, 0)))

    def forward(carry, cycle):
        summed = jnp.zeros((K, NLON, C), jnp.float32)
        for d in range(3):
            source = lax.dynamic_index_in_dim(padded, cycle + d, 0, keepdims=False).astype(jnp.float32)
            for s in range(NTAP):
                moved = jnp.roll(source, -offsets[cycle, d, s], axis=0)
                summed = summed + filter_values[:, cycle, d, s][:, None, None] * moved[None]
        filtered = summed.astype(jnp.bfloat16)
        mixed = jnp.dot(filtered[0], mixing[0], preferred_element_type=jnp.float32)
        for k in range(1, K):
            mixed = mixed + jnp.dot(filtered[k], mixing[k], preferred_element_type=jnp.float32)
        state_row = lax.dynamic_index_in_dim(state, cycle, 0, keepdims=False).astype(jnp.float32)
        out_row = (state_row + gelu_value(mixed)).astype(jnp.bfloat16)
        cot_row = lax.dynamic_index_in_dim(cotangent, cycle, 0, keepdims=False).astype(jnp.float32)
        slope_row = (cot_row * gelu_slope(mixed)).astype(jnp.bfloat16)
        terms = jnp.stack([jnp.dot(filtered[k].T, slope_row, preferred_element_type=jnp.float32) for k in range(K)])
        return (carry + terms, (out_row, slope_row))
    grad_sum, (output, slope) = lax.scan(forward, jnp.zeros((K, C, C), jnp.float32), jnp.arange(NLAT, dtype=jnp.int32))
    mixing_grad = grad_sum / jnp.sqrt(jnp.float32(NLAT * NLON))
    slope_pad = jnp.pad(slope, ((1, 1), (0, 0), (0, 0)))

    def backward(cycle):
        summed = jnp.zeros((K, NLON, C), jnp.float32)
        for d in range(3):
            place = cycle + 2 - d
            source = lax.dynamic_index_in_dim(slope_pad, place, 0, keepdims=False).astype(jnp.float32)
            for s in range(NTAP):
                moved = jnp.roll(source, off_pad[place, d, s], axis=0)
                summed = summed + psi_pad[:, place, d, s][:, None, None] * moved[None]
        spread = summed.astype(jnp.bfloat16)
        cot_row = lax.dynamic_index_in_dim(cotangent, cycle, 0, keepdims=False).astype(jnp.float32)
        for k in range(K):
            cot_row = cot_row + jnp.dot(spread[k], mixing[k].T, preferred_element_type=jnp.float32)
        return cot_row.astype(jnp.bfloat16)
    state_grad = lax.map(backward, jnp.arange(NLAT, dtype=jnp.int32))
    return (output, mixing_grad, state_grad)
```

```python
import functools
import math

import jax
import jax.numpy as jnp
import numpy as np
from jax import lax
from jax.experimental import pallas as pl
from jax.experimental.pallas import tpu as pltpu
from jax.sharding import PartitionSpec as P

HALO = 16
POLAR = 1
TJ = 128
WIN = TJ + 2 * HALO
SPAN = 512
F32 = jnp.float32
BF16 = jnp.bfloat16
VMEM_LIMIT = 50 * 1024 * 1024


def widen(shard, padded_width):
    lat, lon = lax.axis_size("lat"), lax.axis_size("lon")
    up = [(i, i + 1) for i in range(lat - 1)]
    down = [(i + 1, i) for i in range(lat - 1)]
    before = lax.ppermute(shard[-1:], "lat", up)
    after = lax.ppermute(shard[:1], "lat", down)
    rows = jnp.concatenate([before, shard, after], axis=0)
    right = [(i, (i + 1) % lon) for i in range(lon)]
    left = [((i + 1) % lon, i) for i in range(lon)]
    west = lax.ppermute(rows[:, -HALO:], "lon", right)
    east = lax.ppermute(rows[:, :HALO], "lon", left)
    fill = padded_width - shard.shape[1]
    parts = [west, rows, east]
    if fill:
        parts.append(jnp.zeros((rows.shape[0], fill, shard.shape[2]), shard.dtype))
    return jnp.concatenate(parts, axis=1)


def base_rows(psi_loc, off_loc, polar_pad, rows, adjoint):
    targets = np.arange(rows)
    places = jnp.arange(SPAN, dtype=jnp.int32)
    total = None
    for d in range(3):
        wrow = targets + (2 - d if adjoint else 1)
        window = 2 - d if adjoint else d
        w = psi_loc[:, wrow, d, :] * (1.0 - polar_pad[wrow])[None, :, None]
        off = off_loc[wrow, d, :]
        off = jnp.clip(-off if adjoint else off, -HALO, HALO) + HALO + window * WIN
        hit = (off[:, :, None] == places[None, None, :]).astype(F32)
        term = jnp.sum(w[..., None] * hit[None], axis=2)
        total = term if total is None else total + term
    total = jnp.transpose(total, (1, 0, 2))
    return jnp.pad(total, ((0, 0), (0, 5), (0, 0)))


def polar_kernel(pairs, ntgt, cycle, blocks, flag_ref, start_ref, w_ref, g_ref, out_ref, buf):
    extra = blocks * TJ
    chans = g_ref.shape[2]

    @pl.when(flag_ref[0] > 0)
    def _():
        for e in range(g_ref.shape[0]):

            @pl.loop(0, cycle // 16)
            def _(i):
                at = pl.multiple_of(i * 16, 16)
                buf[e, pl.ds(at, 16), :] = g_ref[e, pl.ds(at, 16), :].astype(F32)

            @pl.loop(0, extra // 16)
            def _(i):
                at = pl.multiple_of(i * 16, 16)
                buf[e, pl.ds(cycle + at, 16), :] = g_ref[e, pl.ds(at, 16), :].astype(F32)

        for t in range(ntgt):

            @pl.loop(0, extra // 16)
            def _(i):
                at = pl.multiple_of(i * 16, 16)
                acc = [jnp.zeros((16, chans), F32) for _ in range(3)]
                for p, (tgt, e) in enumerate(pairs):
                    if tgt != t:
                        continue
                    for s in range(8):
                        start = start_ref[p * 8 + s]
                        low = pl.multiple_of(start // 8 * 8 + at, 8)
                        x = buf[e, pl.ds(low, 24), :]
                        x = pltpu.roll(x, lax.rem(24 - lax.rem(start, 8), 24), 0)[:16]
                        for k in range(3):
                            acc[k] = acc[k] + w_ref[(p * 3 + k) * 8 + s] * x
                for k in range(3):
                    out_ref[t * 3 + k, pl.ds(at, 16), :] = acc[k]


def polar_terms(gathered, flag, starts, weights, pairs, ntgt, padded_width):
    ns, cycle, chans = gathered.shape
    smem = pl.BlockSpec(memory_space=pltpu.SMEM)
    vmem = pl.BlockSpec(memory_space=pltpu.VMEM)
    return pl.pallas_call(
        functools.partial(polar_kernel, pairs, ntgt, cycle, padded_width // TJ),
        out_shape=jax.ShapeDtypeStruct((ntgt * 3, padded_width, chans), F32),
        in_specs=[smem, smem, smem, vmem],
        out_specs=vmem,
        scratch_shapes=[pltpu.VMEM((ns, cycle + padded_width, chans), F32)],
        compiler_params=pltpu.CompilerParams(vmem_limit_bytes=VMEM_LIMIT),
        name="polar",
    )(flag, starts.reshape(-1), weights.reshape(-1), gathered)


def filter_row(slot_ref, base_ref, srcs, extra_ref, band, src, filt, blocks):
    r = pl.program_id(0)
    chans = src.shape[1]
    src[3 * WIN :, :] = jnp.zeros((SPAN - 3 * WIN, chans), BF16)
    for k in range(3):
        row = jnp.broadcast_to(base_ref[0, k : k + 1, :], (TJ, SPAN))
        moved = pltpu.roll(row, 0, 1, stride=1, stride_axis=0)
        band[k * TJ : (k + 1) * TJ, :] = moved.astype(BF16)
    for b in range(blocks):
        for e in range(3):
            src[e * WIN : (e + 1) * WIN, :] = srcs[e][0, b * TJ : b * TJ + WIN, :]
        acc = jnp.dot(band[...], src[...], preferred_element_type=F32)
        here = slice(b * TJ, (b + 1) * TJ)
        for k in range(3):
            filt[here, k * chans : (k + 1) * chans] = acc[k * TJ : (k + 1) * TJ].astype(BF16)

        @pl.when(slot_ref[r] >= 0)
        def _():
            for k in range(3):
                whole = acc[k * TJ : (k + 1) * TJ] + extra_ref[k, here, :]
                filt[here, k * chans : (k + 1) * chans] = whole.astype(BF16)


def forward_kernel(blocks, slot_ref, base_ref, s0, s1, s2, extra_ref, mix_ref, state_ref, cot_ref,
                   out_ref, slope_ref, filt_ref, band, src):
    width = state_ref.shape[1]
    filt = filt_ref.at[0]
    filter_row(slot_ref, base_ref, (s0, s1, s2), extra_ref, band, src, filt, blocks)
    padded = blocks * TJ
    if padded > width:
        low = width // 16 * 16
        slope_ref[0, low:, :] = jnp.zeros((padded - low, slope_ref.shape[2]), BF16)
    for b in range(blocks):
        at, n = b * TJ, min(TJ, width - b * TJ)
        mixed = jnp.dot(filt[at : at + TJ, :], mix_ref[...], preferred_element_type=F32)[:n]
        rising = 0.5 * (1.0 + lax.erf(mixed * 0.7071067811865476))
        bump = mixed * jnp.exp(-0.5 * mixed * mixed) * 0.3989422804014327
        x = state_ref[0, at : at + n, :].astype(F32)
        g = cot_ref[0, at : at + n, :].astype(F32)
        out_ref[0, at : at + n, :] = (x + mixed * rising).astype(BF16)
        slope_ref[0, at : at + n, :] = (g * (rising + bump)).astype(BF16)


def backward_kernel(blocks, slot_ref, base_ref, s0, s1, s2, extra_ref, mix_ref, cot_ref,
                    grad_ref, band, src, filt):
    width = cot_ref.shape[1]
    filter_row(slot_ref, base_ref, (s0, s1, s2), extra_ref, band, src, filt, blocks)
    back = jnp.dot(filt[...], mix_ref[...], preferred_element_type=F32)[:width]
    grad_ref[0] = (cot_ref[0].astype(F32) + back).astype(BF16)


def grad_kernel(scale, filt_ref, slope_ref, out_ref):
    r = pl.program_id(0)
    term = lax.dot_general(
        filt_ref[0], slope_ref[0], (((0,), (0,)), ((), ())), preferred_element_type=F32
    )

    @pl.when(r == 0)
    def _():
        out_ref[...] = term

    @pl.when(r > 0)
    def _():
        out_ref[...] += term

    @pl.when(r == pl.num_programs(0) - 1)
    def _():
        out_ref[...] *= scale


def conv_specs(wl, padded, chans):
    one = lambda e: pl.BlockSpec((1, wl, chans), lambda r, slot, e=e: (r + e, 0, 0))
    return [
        pl.BlockSpec((1, 8, SPAN), lambda r, slot: (r, 0, 0)),
        one(0),
        one(1),
        one(2),
        pl.BlockSpec((3, padded, chans), lambda r, slot: (jnp.maximum(slot[r], 0), 0, 0)),
        pl.BlockSpec((3 * chans, chans), lambda r, slot: (0, 0)),
    ]


def per_device(state, filter_values, offsets, mixing, cotangent):
    rows, width, chans = state.shape
    nrings = offsets.shape[0]
    nlat, nlon = lax.axis_size("lat"), lax.axis_size("lon")
    cycle = width * nlon
    blocks = -(-width // TJ)
    padded = blocks * TJ
    wl = padded + 2 * HALO
    lat_id = lax.axis_index("lat")
    lat_start = lat_id * rows
    lon_start = lax.axis_index("lon") * width
    psi_pad = jnp.pad(filter_values, ((0, 0), (1, 1), (0, 0), (0, 0)))
    off_pad = jnp.pad(offsets, ((1, 1), (0, 0), (0, 0)))
    psi_loc = lax.dynamic_slice_in_dim(psi_pad, lat_start, rows + 2, 1)
    off_loc = lax.dynamic_slice_in_dim(off_pad, lat_start, rows + 2, 0)
    ring = lat_start + jnp.arange(rows + 2, dtype=jnp.int32) - 1
    polar_pad = ((ring < POLAR) | (ring >= nrings - POLAR)).astype(F32)
    south = lat_id == 0
    north = lat_id == nlat - 1
    flag = (south | north).astype(jnp.int32)[None]
    row_ids = jnp.arange(rows, dtype=jnp.int32)

    w_pole = jnp.where(south, psi_loc[:, 1], psi_loc[:, rows])
    o_pole = jnp.where(south, off_loc[1], off_loc[rows])
    w_two = jnp.where(south, w_pole[:, 1:3], w_pole[:, 0:2])
    o_two = jnp.where(south, o_pole[1:3], o_pole[0:2])
    two = jnp.where(south, state[:2], state[-2:])
    gathered = lax.all_gather(two, "lon", axis=1, tiled=True)
    wide = widen(state, padded)
    fwd_extra = polar_terms(
        gathered, flag, (lon_start + o_two) % cycle, jnp.transpose(w_two, (1, 0, 2)),
        [(0, 0), (0, 1)], 1, padded,
    )
    fwd_slot = jnp.where((south & (row_ids == 0)) | (north & (row_ids == rows - 1)), 0, -1).astype(jnp.int32)
    fwd_base = base_rows(psi_loc, off_loc, polar_pad, rows, False)
    field = pl.BlockSpec((1, width, chans), lambda r, slot: (r, 0, 0))
    params = pltpu.CompilerParams(vmem_limit_bytes=VMEM_LIMIT)
    flops = rows * padded * chans * (3 * SPAN + 3 * chans) * 2
    cost = pl.CostEstimate(flops=flops, bytes_accessed=rows * padded * chans * 20, transcendentals=0)
    output, slope, filtered = pl.pallas_call(
        functools.partial(forward_kernel, blocks),
        out_shape=(
            jax.ShapeDtypeStruct(state.shape, BF16),
            jax.ShapeDtypeStruct((rows, padded, chans), BF16),
            jax.ShapeDtypeStruct((rows, padded, 3 * chans), BF16),
        ),
        grid_spec=pltpu.PrefetchScalarGridSpec(
            num_scalar_prefetch=1,
            grid=(rows,),
            in_specs=conv_specs(wl, padded, chans) + [field, field],
            out_specs=(
                field,
                pl.BlockSpec((1, padded, chans), lambda r, slot: (r, 0, 0)),
                pl.BlockSpec((1, padded, 3 * chans), lambda r, slot: (r, 0, 0)),
            ),
            scratch_shapes=[pltpu.VMEM((3 * TJ, SPAN), BF16), pltpu.VMEM((SPAN, chans), BF16)],
        ),
        compiler_params=params,
        cost_estimate=cost,
        name="forward",
    )(fwd_slot, fwd_base, wide, wide, wide, fwd_extra, mixing.reshape(3 * chans, chans), state, cotangent)

    local_grad = pl.pallas_call(
        functools.partial(grad_kernel, 1.0 / math.sqrt(nrings * cycle)),
        out_shape=jax.ShapeDtypeStruct((3 * chans, chans), F32),
        grid=(rows,),
        in_specs=[
            pl.BlockSpec((1, padded, 3 * chans), lambda r: (r, 0, 0)),
            pl.BlockSpec((1, padded, chans), lambda r: (r, 0, 0)),
        ],
        out_specs=pl.BlockSpec((3 * chans, chans), lambda r: (0, 0)),
        compiler_params=params,
        cost_estimate=cost,
        name="channel_grad",
    )(filtered, slope).reshape(3, chans, chans)
    partial_grad = lax.psum_scatter(local_grad, "lat", scatter_dimension=1, tiled=True)
    mixing_grad = lax.psum_scatter(partial_grad, "lon", scatter_dimension=2, tiled=True)

    slope = slope[:, :width]
    pole_slope = jnp.where(south, slope[:1], slope[-1:])
    pole_cycle = lax.all_gather(pole_slope, "lon", axis=1, tiled=True)
    slope_wide = widen(slope, padded)
    bwd_extra = polar_terms(
        pole_cycle, flag, (lon_start - o_two[::1]) % cycle, jnp.transpose(w_two, (1, 0, 2)),
        [(0, 0), (1, 0)], 2, padded,
    )
    first = jnp.where(south, 0, rows - 2)
    bwd_slot = jnp.where(
        flag[0] * ((row_ids >= first) & (row_ids < first + 2)) > 0, row_ids - first, -1
    ).astype(jnp.int32)
    bwd_base = base_rows(psi_loc, off_loc, polar_pad, rows, True)
    state_grad = pl.pallas_call(
        functools.partial(backward_kernel, blocks),
        out_shape=jax.ShapeDtypeStruct(state.shape, BF16),
        grid_spec=pltpu.PrefetchScalarGridSpec(
            num_scalar_prefetch=1,
            grid=(rows,),
            in_specs=conv_specs(wl, padded, chans) + [field],
            out_specs=field,
            scratch_shapes=[
                pltpu.VMEM((3 * TJ, SPAN), BF16),
                pltpu.VMEM((SPAN, chans), BF16),
                pltpu.VMEM((padded, 3 * chans), BF16),
            ],
        ),
        compiler_params=params,
        cost_estimate=cost,
        name="backward",
    )(bwd_slot, bwd_base, slope_wide, slope_wide, slope_wide, bwd_extra,
      jnp.swapaxes(mixing, 1, 2).reshape(3 * chans, chans), cotangent)
    return (output, mixing_grad, state_grad)


def solution(mesh):
    in_specs = (P("lat", "lon", None), P(), P(), P(), P("lat", "lon", None))
    out_specs = (P("lat", "lon", None), P(None, "lat", "lon"), P("lat", "lon", None))
    return jax.shard_map(
        per_device, mesh=mesh, in_specs=in_specs, out_specs=out_specs, check_vma=False
    )
```

```python
import functools
import math

import jax
import jax.numpy as jnp
import numpy as np
from jax import lax
from jax.experimental import pallas as pl
from jax.experimental.pallas import tpu as pltpu
from jax.sharding import PartitionSpec as P

HALO = 16
POLAR = 1
TJ = 128
WIN = TJ + 2 * HALO
SPAN = 512
F32 = jnp.float32
BF16 = jnp.bfloat16
VMEM_LIMIT = 50 * 1024 * 1024


def widen(shard, padded_width):
    lat, lon = lax.axis_size("lat"), lax.axis_size("lon")
    up = [(i, i + 1) for i in range(lat - 1)]
    down = [(i + 1, i) for i in range(lat - 1)]
    before = lax.ppermute(shard[-1:], "lat", up)
    after = lax.ppermute(shard[:1], "lat", down)
    rows = jnp.concatenate([before, shard, after], axis=0)
    right = [(i, (i + 1) % lon) for i in range(lon)]
    left = [((i + 1) % lon, i) for i in range(lon)]
    west = lax.ppermute(rows[:, -HALO:], "lon", right)
    east = lax.ppermute(rows[:, :HALO], "lon", left)
    fill = padded_width - shard.shape[1]
    parts = [west, rows, east]
    if fill:
        parts.append(jnp.zeros((rows.shape[0], fill, shard.shape[2]), shard.dtype))
    return jnp.concatenate(parts, axis=1)


def scatter_sum(local):
    k, chans, _ = local.shape
    nlat, nlon = lax.axis_size("lat"), lax.axis_size("lon")
    left = local.reshape(k, nlat, chans // nlat, nlon, chans // nlon)
    left = jnp.transpose(left, (3, 1, 0, 2, 4))
    for dim, axis in enumerate(("lon", "lat")):
        count = lax.axis_size(axis)
        index = lax.axis_index(axis)
        if count & (count - 1):
            left = lax.psum_scatter(left, axis, scatter_dimension=dim, tiled=True)
            left = lax.squeeze(left, (dim,)) if dim == 0 else left[0]
            continue
        step = 1
        while step < count:
            halves = left.reshape((left.shape[0] // 2, 2) + left.shape[1:])
            bit = index // step % 2
            mine = lax.dynamic_index_in_dim(halves, bit, 1, keepdims=False)
            theirs = lax.dynamic_index_in_dim(halves, 1 - bit, 1, keepdims=False)
            if (axis == "lon") == (step > 1):
                theirs = theirs.astype(BF16)
            got = lax.ppermute(theirs, axis, [(i, i ^ step) for i in range(count)])
            left = mine + got.astype(F32)
            step *= 2
        left = left[0]
    return left


def base_rows(psi_loc, off_loc, polar_pad, rows, adjoint):
    targets = np.arange(rows)
    places = jnp.arange(SPAN, dtype=jnp.int32)
    total = None
    for d in range(3):
        wrow = targets + (2 - d if adjoint else 1)
        window = 2 - d if adjoint else d
        w = psi_loc[:, wrow, d, :] * (1.0 - polar_pad[wrow])[None, :, None]
        off = off_loc[wrow, d, :]
        off = jnp.clip(-off if adjoint else off, -HALO, HALO) + HALO + window * WIN
        hit = (off[:, :, None] == places[None, None, :]).astype(F32)
        term = jnp.sum(w[..., None] * hit[None], axis=2)
        total = term if total is None else total + term
    total = jnp.transpose(total, (1, 0, 2))
    return jnp.pad(total, ((0, 0), (0, 5), (0, 0)))


def polar_kernel(pairs, ntgt, cycle, blocks, flag_ref, start_ref, w_ref, g_ref, out_ref, buf):
    extra = blocks * TJ
    chans = g_ref.shape[2]

    @pl.when(flag_ref[0] > 0)
    def _():
        for e in range(g_ref.shape[0]):

            @pl.loop(0, cycle // 16)
            def _(i):
                at = pl.multiple_of(i * 16, 16)
                buf[e, pl.ds(at, 16), :] = g_ref[e, pl.ds(at, 16), :].astype(F32)

            @pl.loop(0, extra // 16)
            def _(i):
                at = pl.multiple_of(i * 16, 16)
                buf[e, pl.ds(cycle + at, 16), :] = g_ref[e, pl.ds(at, 16), :].astype(F32)

        for t in range(ntgt):

            @pl.loop(0, extra // 16)
            def _(i):
                at = pl.multiple_of(i * 16, 16)
                acc = [jnp.zeros((16, chans), F32) for _ in range(3)]
                for p, (tgt, e) in enumerate(pairs):
                    if tgt != t:
                        continue
                    for s in range(8):
                        start = start_ref[p * 8 + s]
                        low = pl.multiple_of(start // 8 * 8 + at, 8)
                        x = buf[e, pl.ds(low, 24), :]
                        x = pltpu.roll(x, lax.rem(24 - lax.rem(start, 8), 24), 0)[:16]
                        for k in range(3):
                            acc[k] = acc[k] + w_ref[(p * 3 + k) * 8 + s] * x
                for k in range(3):
                    out_ref[t * 3 + k, pl.ds(at, 16), :] = acc[k]


def polar_terms(gathered, flag, starts, weights, pairs, ntgt, padded_width):
    ns, cycle, chans = gathered.shape
    smem = pl.BlockSpec(memory_space=pltpu.SMEM)
    vmem = pl.BlockSpec(memory_space=pltpu.VMEM)
    return pl.pallas_call(
        functools.partial(polar_kernel, pairs, ntgt, cycle, padded_width // TJ),
        out_shape=jax.ShapeDtypeStruct((ntgt * 3, padded_width, chans), F32),
        in_specs=[smem, smem, smem, vmem],
        out_specs=vmem,
        scratch_shapes=[pltpu.VMEM((ns, cycle + padded_width, chans), F32)],
        compiler_params=pltpu.CompilerParams(vmem_limit_bytes=VMEM_LIMIT),
        name="polar",
    )(flag, starts.reshape(-1), weights.reshape(-1), gathered)


def filter_row(at, slot_ref, base_ref, srcs, extra_ref, band, src, filt, blocks):
    r = pl.program_id(0) + at
    chans = src.shape[1]
    src[3 * WIN :, :] = jnp.zeros((SPAN - 3 * WIN, chans), BF16)
    for k in range(3):
        row = jnp.broadcast_to(base_ref[0, k : k + 1, :], (TJ, SPAN))
        moved = pltpu.roll(row, 0, 1, stride=1, stride_axis=0)
        band[k * TJ : (k + 1) * TJ, :] = moved.astype(BF16)
    for b in range(blocks):
        for e in range(3):
            src[e * WIN : (e + 1) * WIN, :] = srcs[e][0, b * TJ : b * TJ + WIN, :]
        acc = jnp.dot(band[...], src[...], preferred_element_type=F32)
        here = slice(b * TJ, (b + 1) * TJ)
        for k in range(3):
            filt[here, k * chans : (k + 1) * chans] = acc[k * TJ : (k + 1) * TJ].astype(BF16)

        @pl.when(slot_ref[r] >= 0)
        def _():
            for k in range(3):
                whole = acc[k * TJ : (k + 1) * TJ] + extra_ref[k, here, :]
                filt[here, k * chans : (k + 1) * chans] = whole.astype(BF16)


def forward_kernel(blocks, slot_ref, base_ref, s0, s1, s2, extra_ref, mix_ref, state_ref, cot_ref,
                   out_ref, slope_ref, filt_ref, band, src):
    width = state_ref.shape[1]
    filt = filt_ref.at[0]
    filter_row(0, slot_ref, base_ref, (s0, s1, s2), extra_ref, band, src, filt, blocks)
    for b in range(blocks):
        at, n = b * TJ, min(TJ, width - b * TJ)
        mixed = jnp.dot(filt[at : at + TJ, :], mix_ref[...], preferred_element_type=F32)[:n]
        rising = 0.5 * (1.0 + lax.erf(mixed * 0.7071067811865476))
        bump = mixed * jnp.exp(-0.5 * mixed * mixed) * 0.3989422804014327
        x = state_ref[0, at : at + n, :].astype(F32)
        g = cot_ref[0, at : at + n, :].astype(F32)
        out_ref[0, at : at + n, :] = (x + mixed * rising).astype(BF16)
        slope_ref[0, at : at + n, :] = (g * (rising + bump)).astype(BF16)


def backward_kernel(blocks, at, slot_ref, base_ref, s0, s1, s2, extra_ref, mix_ref, cot_ref, *rest):
    grad_ref, band, src, filt = rest[-4:]
    width = cot_ref.shape[1]
    filter_row(at, slot_ref, base_ref, (s0, s1, s2), extra_ref, band, src, filt, blocks)
    back = jnp.dot(filt[...], mix_ref[...], preferred_element_type=F32)[:width]
    grad_ref[0] = (cot_ref[0].astype(F32) + back).astype(BF16)


def grad_kernel(scale, filt_ref, slope_ref, out_ref):
    r = pl.program_id(0)
    term = lax.dot_general(
        filt_ref[0, : slope_ref.shape[1], :], slope_ref[0], (((0,), (0,)), ((), ())), preferred_element_type=F32
    )

    @pl.when(r == 0)
    def _():
        out_ref[...] = term

    @pl.when(r > 0)
    def _():
        out_ref[...] += term

    @pl.when(r == pl.num_programs(0) - 1)
    def _():
        out_ref[...] *= scale


def conv_specs(wl, padded, chans, at=0):
    one = lambda e: pl.BlockSpec((1, wl, chans), lambda r, slot, e=e: (r + at + e, 0, 0))
    return [
        pl.BlockSpec((1, 8, SPAN), lambda r, slot: (r + at, 0, 0)),
        one(0),
        one(1),
        one(2),
        pl.BlockSpec((3, padded, chans), lambda r, slot: (jnp.maximum(slot[r + at], 0), 0, 0)),
        pl.BlockSpec((3 * chans, chans), lambda r, slot: (0, 0)),
    ]


def per_device(state, filter_values, offsets, mixing, cotangent):
    rows, width, chans = state.shape
    nrings = offsets.shape[0]
    nlat, nlon = lax.axis_size("lat"), lax.axis_size("lon")
    cycle = width * nlon
    blocks = -(-width // TJ)
    padded = blocks * TJ
    wl = padded + 2 * HALO
    lat_id = lax.axis_index("lat")
    lat_start = lat_id * rows
    lon_start = lax.axis_index("lon") * width
    psi_pad = jnp.pad(filter_values, ((0, 0), (1, 1), (0, 0), (0, 0)))
    off_pad = jnp.pad(offsets, ((1, 1), (0, 0), (0, 0)))
    psi_loc = lax.dynamic_slice_in_dim(psi_pad, lat_start, rows + 2, 1)
    off_loc = lax.dynamic_slice_in_dim(off_pad, lat_start, rows + 2, 0)
    ring = lat_start + jnp.arange(rows + 2, dtype=jnp.int32) - 1
    polar_pad = ((ring < POLAR) | (ring >= nrings - POLAR)).astype(F32)
    south = lat_id == 0
    north = lat_id == nlat - 1
    flag = (south | north).astype(jnp.int32)[None]
    row_ids = jnp.arange(rows, dtype=jnp.int32)

    w_pole = jnp.where(south, psi_loc[:, 1], psi_loc[:, rows])
    o_pole = jnp.where(south, off_loc[1], off_loc[rows])
    w_two = jnp.where(south, w_pole[:, 1:3], w_pole[:, 0:2])
    o_two = jnp.where(south, o_pole[1:3], o_pole[0:2])
    two = jnp.where(south, state[:2], state[-2:])
    gathered = lax.all_gather(two, "lon", axis=1, tiled=True)
    wide = widen(state, padded)
    fwd_extra = polar_terms(
        gathered, flag, (lon_start + o_two) % cycle, jnp.transpose(w_two, (1, 0, 2)),
        [(0, 0), (0, 1)], 1, padded,
    )
    fwd_slot = jnp.where((south & (row_ids == 0)) | (north & (row_ids == rows - 1)), 0, -1).astype(jnp.int32)
    fwd_base = base_rows(psi_loc, off_loc, polar_pad, rows, False)
    field = pl.BlockSpec((1, width, chans), lambda r, slot: (r, 0, 0))
    params = pltpu.CompilerParams(vmem_limit_bytes=VMEM_LIMIT)
    flops = rows * padded * chans * (3 * SPAN + 3 * chans) * 2
    cost = pl.CostEstimate(flops=flops, bytes_accessed=rows * padded * chans * 20, transcendentals=0)
    output, slope, filtered = pl.pallas_call(
        functools.partial(forward_kernel, blocks),
        out_shape=(
            jax.ShapeDtypeStruct(state.shape, BF16),
            jax.ShapeDtypeStruct(state.shape, BF16),
            jax.ShapeDtypeStruct((rows, padded, 3 * chans), BF16),
        ),
        grid_spec=pltpu.PrefetchScalarGridSpec(
            num_scalar_prefetch=1,
            grid=(rows,),
            in_specs=conv_specs(wl, padded, chans) + [field, field],
            out_specs=(
                field,
                field,
                pl.BlockSpec((1, padded, 3 * chans), lambda r, slot: (r, 0, 0)),
            ),
            scratch_shapes=[pltpu.VMEM((3 * TJ, SPAN), BF16), pltpu.VMEM((SPAN, chans), BF16)],
        ),
        compiler_params=params,
        cost_estimate=cost,
        name="forward",
    )(fwd_slot, fwd_base, wide, wide, wide, fwd_extra, mixing.reshape(3 * chans, chans), state, cotangent)

    local_grad = pl.pallas_call(
        functools.partial(grad_kernel, 1.0 / math.sqrt(nrings * cycle)),
        out_shape=jax.ShapeDtypeStruct((3 * chans, chans), F32),
        grid=(rows,),
        in_specs=[
            pl.BlockSpec((1, padded, 3 * chans), lambda r: (r, 0, 0)),
            pl.BlockSpec((1, width, chans), lambda r: (r, 0, 0)),
        ],
        out_specs=pl.BlockSpec((3 * chans, chans), lambda r: (0, 0)),
        compiler_params=params,
        cost_estimate=cost,
        name="channel_grad",
    )(filtered, slope).reshape(3, chans, chans)
    mixing_grad = scatter_sum(local_grad)

    pole_slope = jnp.where(south, slope[:1], slope[-1:])
    pole_cycle = lax.all_gather(pole_slope, "lon", axis=1, tiled=True)
    slope_wide = widen(slope, padded)
    bwd_extra = polar_terms(
        pole_cycle, flag, (lon_start - o_two) % cycle, jnp.transpose(w_two, (1, 0, 2)),
        [(0, 0), (1, 0)], 2, padded,
    )
    first = jnp.where(south, 0, rows - 2)
    bwd_slot = jnp.where(
        flag[0] * ((row_ids >= first) & (row_ids < first + 2)) > 0, row_ids - first, -1
    ).astype(jnp.int32)
    bwd_base = base_rows(psi_loc, off_loc, polar_pad, rows, True)
    mix_t = jnp.swapaxes(mixing, 1, 2).reshape(3 * chans, chans)
    pieces = 3 if rows % 3 == 0 else 1
    part = rows // pieces
    state_grad = None
    for piece in range(pieces):
        at = piece * part
        moved = pl.BlockSpec((1, width, chans), lambda r, slot, at=at: (r + at, 0, 0))
        held = [] if state_grad is None else [state_grad]
        state_grad = pl.pallas_call(
            functools.partial(backward_kernel, blocks, at),
            out_shape=jax.ShapeDtypeStruct(state.shape, BF16),
            grid_spec=pltpu.PrefetchScalarGridSpec(
                num_scalar_prefetch=1,
                grid=(part,),
                in_specs=conv_specs(wl, padded, chans, at) + [moved]
                + [pl.BlockSpec(memory_space=pl.ANY)] * len(held),
                out_specs=moved,
                scratch_shapes=[
                    pltpu.VMEM((3 * TJ, SPAN), BF16),
                    pltpu.VMEM((SPAN, chans), BF16),
                    pltpu.VMEM((padded, 3 * chans), BF16),
                ],
            ),
            input_output_aliases={8: 0} if held else {},
            compiler_params=params,
            cost_estimate=pl.CostEstimate(
                flops=flops // pieces,
                bytes_accessed=rows * padded * chans * 20 // pieces,
                transcendentals=0,
            ),
            name="backward_%d" % piece,
        )(bwd_slot, bwd_base, slope_wide, slope_wide, slope_wide, bwd_extra, mix_t, cotangent, *held)
    return (output, mixing_grad, state_grad)


def solution(mesh):
    in_specs = (P("lat", "lon", None), P(), P(), P(), P("lat", "lon", None))
    out_specs = (P("lat", "lon", None), P(None, "lat", "lon"), P("lat", "lon", None))
    return jax.shard_map(
        per_device, mesh=mesh, in_specs=in_specs, out_specs=out_specs, check_vma=False
    )
```

```python
import functools
import math

import jax
import jax.numpy as jnp
import numpy as np
from jax import lax
from jax.experimental import pallas as pl
from jax.experimental.pallas import tpu as pltpu
from jax.sharding import PartitionSpec as P

HALO = 16
POLAR = 1
TJ = 128
WIN = TJ + 2 * HALO
SPAN = 512
F32 = jnp.float32
BF16 = jnp.bfloat16
VMEM_LIMIT = 50 * 1024 * 1024


def widen(shard, padded_width):
    lat, lon = lax.axis_size("lat"), lax.axis_size("lon")
    up = [(i, i + 1) for i in range(lat - 1)]
    down = [(i + 1, i) for i in range(lat - 1)]
    before = lax.ppermute(shard[-1:], "lat", up)
    after = lax.ppermute(shard[:1], "lat", down)
    rows = jnp.concatenate([before, shard, after], axis=0)
    right = [(i, (i + 1) % lon) for i in range(lon)]
    left = [((i + 1) % lon, i) for i in range(lon)]
    west = lax.ppermute(rows[:, -HALO:], "lon", right)
    east = lax.ppermute(rows[:, :HALO], "lon", left)
    fill = padded_width - shard.shape[1]
    parts = [west, rows, east]
    if fill:
        parts.append(jnp.zeros((rows.shape[0], fill, shard.shape[2]), shard.dtype))
    return jnp.concatenate(parts, axis=1)


def scatter_sum(left):
    for dim, axis in enumerate(("lon", "lat")):
        count = lax.axis_size(axis)
        index = lax.axis_index(axis)
        if count & (count - 1):
            left = lax.psum_scatter(left, axis, scatter_dimension=dim, tiled=True)
            left = lax.squeeze(left, (dim,)) if dim == 0 else left[0]
            continue
        step = 1
        while step < count:
            halves = left.reshape((left.shape[0] // 2, 2) + left.shape[1:])
            bit = index // step % 2
            mine = lax.dynamic_index_in_dim(halves, bit, 1, keepdims=False)
            theirs = lax.dynamic_index_in_dim(halves, 1 - bit, 1, keepdims=False)
            if (axis == "lon") == (step > 1):
                theirs = theirs.astype(BF16)
            got = lax.ppermute(theirs, axis, [(i, i ^ step) for i in range(count)])
            left = mine + got.astype(F32)
            step *= 2
        left = left[0]
    return left


def base_rows(psi_loc, off_loc, polar_pad, rows, adjoint):
    targets = np.arange(rows)
    places = jnp.arange(SPAN, dtype=jnp.int32)
    total = None
    for d in range(3):
        wrow = targets + (2 - d if adjoint else 1)
        window = 2 - d if adjoint else d
        w = psi_loc[:, wrow, d, :] * (1.0 - polar_pad[wrow])[None, :, None]
        off = off_loc[wrow, d, :]
        off = jnp.clip(-off if adjoint else off, -HALO, HALO) + HALO + window * WIN
        hit = (off[:, :, None] == places[None, None, :]).astype(F32)
        term = jnp.sum(w[..., None] * hit[None], axis=2)
        total = term if total is None else total + term
    total = jnp.transpose(total, (1, 0, 2))
    return jnp.pad(total, ((0, 0), (0, 5), (0, 0)))


def polar_kernel(pairs, ntgt, cycle, blocks, flag_ref, start_ref, w_ref, g_ref, out_ref, buf):
    extra = blocks * TJ
    chans = g_ref.shape[2]

    @pl.when(flag_ref[0] > 0)
    def _():
        for e in range(g_ref.shape[0]):

            @pl.loop(0, cycle // 16)
            def _(i):
                at = pl.multiple_of(i * 16, 16)
                buf[e, pl.ds(at, 16), :] = g_ref[e, pl.ds(at, 16), :].astype(F32)

            @pl.loop(0, extra // 16)
            def _(i):
                at = pl.multiple_of(i * 16, 16)
                buf[e, pl.ds(cycle + at, 16), :] = g_ref[e, pl.ds(at, 16), :].astype(F32)

        for t in range(ntgt):

            @pl.loop(0, extra // 16)
            def _(i):
                at = pl.multiple_of(i * 16, 16)
                acc = [jnp.zeros((16, chans), F32) for _ in range(3)]
                for p, (tgt, e) in enumerate(pairs):
                    if tgt != t:
                        continue
                    for s in range(8):
                        start = start_ref[p * 8 + s]
                        low = pl.multiple_of(start // 8 * 8 + at, 8)
                        x = buf[e, pl.ds(low, 24), :]
                        x = pltpu.roll(x, lax.rem(24 - lax.rem(start, 8), 24), 0)[:16]
                        for k in range(3):
                            acc[k] = acc[k] + w_ref[(p * 3 + k) * 8 + s] * x
                for k in range(3):
                    out_ref[t * 3 + k, pl.ds(at, 16), :] = acc[k]


def polar_terms(gathered, flag, starts, weights, pairs, ntgt, padded_width):
    ns, cycle, chans = gathered.shape
    smem = pl.BlockSpec(memory_space=pltpu.SMEM)
    vmem = pl.BlockSpec(memory_space=pltpu.VMEM)
    return pl.pallas_call(
        functools.partial(polar_kernel, pairs, ntgt, cycle, padded_width // TJ),
        out_shape=jax.ShapeDtypeStruct((ntgt * 3, padded_width, chans), F32),
        in_specs=[smem, smem, smem, vmem],
        out_specs=vmem,
        scratch_shapes=[pltpu.VMEM((ns, cycle + padded_width, chans), F32)],
        compiler_params=pltpu.CompilerParams(vmem_limit_bytes=VMEM_LIMIT),
        name="polar",
    )(flag, starts.reshape(-1), weights.reshape(-1), gathered)


def filter_row(at, slot_ref, base_ref, srcs, extra_ref, band, src, filt, blocks):
    r = pl.program_id(0) + at
    chans = src.shape[1]
    src[3 * WIN :, :] = jnp.zeros((SPAN - 3 * WIN, chans), BF16)
    for k in range(3):
        row = jnp.broadcast_to(base_ref[0, k : k + 1, :], (TJ, SPAN))
        moved = pltpu.roll(row, 0, 1, stride=1, stride_axis=0)
        band[k * TJ : (k + 1) * TJ, :] = moved.astype(BF16)
    for b in range(blocks):
        for e in range(3):
            src[e * WIN : (e + 1) * WIN, :] = srcs[e][0, b * TJ : b * TJ + WIN, :]
        acc = jnp.dot(band[...], src[...], preferred_element_type=F32)
        here = slice(b * TJ, (b + 1) * TJ)
        for k in range(3):
            filt[here, k * chans : (k + 1) * chans] = acc[k * TJ : (k + 1) * TJ].astype(BF16)

        @pl.when(slot_ref[r] >= 0)
        def _():
            for k in range(3):
                whole = acc[k * TJ : (k + 1) * TJ] + extra_ref[k, here, :]
                filt[here, k * chans : (k + 1) * chans] = whole.astype(BF16)


def forward_kernel(blocks, slot_ref, base_ref, s0, s1, s2, extra_ref, mix_ref, state_ref, cot_ref,
                   out_ref, slope_ref, filt_ref, band, src):
    width = state_ref.shape[1]
    filt = filt_ref.at[0]
    filter_row(0, slot_ref, base_ref, (s0, s1, s2), extra_ref, band, src, filt, blocks)
    for b in range(blocks):
        at, n = b * TJ, min(TJ, width - b * TJ)
        mixed = jnp.dot(filt[at : at + TJ, :], mix_ref[...], preferred_element_type=F32)[:n]
        rising = 0.5 * (1.0 + lax.erf(mixed * 0.7071067811865476))
        bump = mixed * jnp.exp(-0.5 * mixed * mixed) * 0.3989422804014327
        x = state_ref[0, at : at + n, :].astype(F32)
        g = cot_ref[0, at : at + n, :].astype(F32)
        out_ref[0, at : at + n, :] = (x + mixed * rising).astype(BF16)
        slope_ref[0, at : at + n, :] = (g * (rising + bump)).astype(BF16)


def backward_kernel(blocks, at, slot_ref, base_ref, s0, s1, s2, extra_ref, mix_ref, cot_ref, *rest):
    grad_ref, band, src, filt = rest[-4:]
    width = cot_ref.shape[1]
    filter_row(at, slot_ref, base_ref, (s0, s1, s2), extra_ref, band, src, filt, blocks)
    back = jnp.dot(filt[...], mix_ref[...], preferred_element_type=F32)[:width]
    grad_ref[0] = (cot_ref[0].astype(F32) + back).astype(BF16)


def grad_kernel(scale, filt_ref, slope_ref, out_ref, total):
    r = pl.program_id(0)
    term = lax.dot_general(
        filt_ref[0, : slope_ref.shape[1], :], slope_ref[0], (((0,), (0,)), ((), ())),
        preferred_element_type=F32,
    )

    @pl.when(r == 0)
    def _():
        total[...] = term

    @pl.when(r > 0)
    def _():
        total[...] += term

    @pl.when(r == pl.num_programs(0) - 1)
    def _():
        if len(out_ref.shape) == 2:
            out_ref[...] = total[...] * scale
            return
        nlon, nlat, _, cr, cc = out_ref.shape
        for q in range(nlon):
            for b in range(nlat):
                for k in range(3):
                    at = (k * nlat + b) * cr
                    out_ref[q, b, k] = total[at : at + cr, q * cc : (q + 1) * cc] * scale


def conv_specs(wl, padded, chans, at=0):
    one = lambda e: pl.BlockSpec((1, wl, chans), lambda r, slot, e=e: (r + at + e, 0, 0))
    return [
        pl.BlockSpec((1, 8, SPAN), lambda r, slot: (r + at, 0, 0)),
        one(0),
        one(1),
        one(2),
        pl.BlockSpec((3, padded, chans), lambda r, slot: (jnp.maximum(slot[r + at], 0), 0, 0)),
        pl.BlockSpec((3 * chans, chans), lambda r, slot: (0, 0)),
    ]


def per_device(state, filter_values, offsets, mixing, cotangent):
    rows, width, chans = state.shape
    nrings = offsets.shape[0]
    nlat, nlon = lax.axis_size("lat"), lax.axis_size("lon")
    cycle = width * nlon
    blocks = -(-width // TJ)
    padded = blocks * TJ
    wl = padded + 2 * HALO
    lat_id = lax.axis_index("lat")
    lat_start = lat_id * rows
    lon_start = lax.axis_index("lon") * width
    psi_pad = jnp.pad(filter_values, ((0, 0), (1, 1), (0, 0), (0, 0)))
    off_pad = jnp.pad(offsets, ((1, 1), (0, 0), (0, 0)))
    psi_loc = lax.dynamic_slice_in_dim(psi_pad, lat_start, rows + 2, 1)
    off_loc = lax.dynamic_slice_in_dim(off_pad, lat_start, rows + 2, 0)
    ring = lat_start + jnp.arange(rows + 2, dtype=jnp.int32) - 1
    polar_pad = ((ring < POLAR) | (ring >= nrings - POLAR)).astype(F32)
    south = lat_id == 0
    north = lat_id == nlat - 1
    flag = (south | north).astype(jnp.int32)[None]
    row_ids = jnp.arange(rows, dtype=jnp.int32)

    w_pole = jnp.where(south, psi_loc[:, 1], psi_loc[:, rows])
    o_pole = jnp.where(south, off_loc[1], off_loc[rows])
    w_two = jnp.where(south, w_pole[:, 1:3], w_pole[:, 0:2])
    o_two = jnp.where(south, o_pole[1:3], o_pole[0:2])
    two = jnp.where(south, state[:2], state[-2:])
    gathered = lax.all_gather(two, "lon", axis=1, tiled=True)
    wide = widen(state, padded)
    fwd_extra = polar_terms(
        gathered, flag, (lon_start + o_two) % cycle, jnp.transpose(w_two, (1, 0, 2)),
        [(0, 0), (0, 1)], 1, padded,
    )
    fwd_slot = jnp.where((south & (row_ids == 0)) | (north & (row_ids == rows - 1)), 0, -1).astype(jnp.int32)
    fwd_base = base_rows(psi_loc, off_loc, polar_pad, rows, False)
    field = pl.BlockSpec((1, width, chans), lambda r, slot: (r, 0, 0))
    params = pltpu.CompilerParams(vmem_limit_bytes=VMEM_LIMIT)
    flops = rows * padded * chans * (3 * SPAN + 3 * chans) * 2
    cost = pl.CostEstimate(flops=flops, bytes_accessed=rows * padded * chans * 20, transcendentals=0)
    output, slope, filtered = pl.pallas_call(
        functools.partial(forward_kernel, blocks),
        out_shape=(
            jax.ShapeDtypeStruct(state.shape, BF16),
            jax.ShapeDtypeStruct(state.shape, BF16),
            jax.ShapeDtypeStruct((rows, padded, 3 * chans), BF16),
        ),
        grid_spec=pltpu.PrefetchScalarGridSpec(
            num_scalar_prefetch=1,
            grid=(rows,),
            in_specs=conv_specs(wl, padded, chans) + [field, field],
            out_specs=(
                field,
                field,
                pl.BlockSpec((1, padded, 3 * chans), lambda r, slot: (r, 0, 0)),
            ),
            scratch_shapes=[pltpu.VMEM((3 * TJ, SPAN), BF16), pltpu.VMEM((SPAN, chans), BF16)],
        ),
        compiler_params=params,
        cost_estimate=cost,
        name="forward",
    )(fwd_slot, fwd_base, wide, wide, wide, fwd_extra, mixing.reshape(3 * chans, chans), state, cotangent)

    cr, cc = chans // nlat, chans // nlon
    direct = cr % 8 == 0 and cc % 128 == 0
    grad_shape = (nlon, nlat, 3, cr, cc) if direct else (3 * chans, chans)
    local_grad = pl.pallas_call(
        functools.partial(grad_kernel, 1.0 / math.sqrt(nrings * cycle)),
        out_shape=jax.ShapeDtypeStruct(grad_shape, F32),
        grid=(rows,),
        in_specs=[
            pl.BlockSpec((1, padded, 3 * chans), lambda r: (r, 0, 0)),
            pl.BlockSpec((1, width, chans), lambda r: (r, 0, 0)),
        ],
        out_specs=pl.BlockSpec(grad_shape, lambda r: (0,) * len(grad_shape)),
        scratch_shapes=[pltpu.VMEM((3 * chans, chans), F32)],
        compiler_params=params,
        cost_estimate=cost,
        name="channel_grad",
    )(filtered, slope)
    if not direct:
        local_grad = local_grad.reshape(3, nlat, cr, nlon, cc)
        local_grad = jnp.transpose(local_grad, (3, 1, 0, 2, 4))
    mixing_grad = scatter_sum(local_grad)

    pole_slope = jnp.where(south, slope[:1], slope[-1:])
    pole_cycle = lax.all_gather(pole_slope, "lon", axis=1, tiled=True)
    slope_wide = widen(slope, padded)
    bwd_extra = polar_terms(
        pole_cycle, flag, (lon_start - o_two) % cycle, jnp.transpose(w_two, (1, 0, 2)),
        [(0, 0), (1, 0)], 2, padded,
    )
    first = jnp.where(south, 0, rows - 2)
    bwd_slot = jnp.where(
        flag[0] * ((row_ids >= first) & (row_ids < first + 2)) > 0, row_ids - first, -1
    ).astype(jnp.int32)
    bwd_base = base_rows(psi_loc, off_loc, polar_pad, rows, True)
    mix_t = jnp.swapaxes(mixing, 1, 2).reshape(3 * chans, chans)
    pieces = 3 if rows % 3 == 0 else 1
    part = rows // pieces
    state_grad = None
    for piece in range(pieces):
        at = piece * part
        moved = pl.BlockSpec((1, width, chans), lambda r, slot, at=at: (r + at, 0, 0))
        held = [] if state_grad is None else [state_grad]
        state_grad = pl.pallas_call(
            functools.partial(backward_kernel, blocks, at),
            out_shape=jax.ShapeDtypeStruct(state.shape, BF16),
            grid_spec=pltpu.PrefetchScalarGridSpec(
                num_scalar_prefetch=1,
                grid=(part,),
                in_specs=conv_specs(wl, padded, chans, at) + [moved]
                + [pl.BlockSpec(memory_space=pl.ANY)] * len(held),
                out_specs=moved,
                scratch_shapes=[
                    pltpu.VMEM((3 * TJ, SPAN), BF16),
                    pltpu.VMEM((SPAN, chans), BF16),
                    pltpu.VMEM((padded, 3 * chans), BF16),
                ],
            ),
            input_output_aliases={8: 0} if held else {},
            compiler_params=params,
            cost_estimate=pl.CostEstimate(
                flops=flops // pieces,
                bytes_accessed=rows * padded * chans * 20 // pieces,
                transcendentals=0,
            ),
            name="backward_%d" % piece,
        )(bwd_slot, bwd_base, slope_wide, slope_wide, slope_wide, bwd_extra, mix_t, cotangent, *held)
    return (output, mixing_grad, state_grad)


def solution(mesh):
    in_specs = (P("lat", "lon", None), P(), P(), P(), P("lat", "lon", None))
    out_specs = (P("lat", "lon", None), P(None, "lat", "lon"), P("lat", "lon", None))
    return jax.shard_map(
        per_device, mesh=mesh, in_specs=in_specs, out_specs=out_specs, check_vma=False
    )
```
